32 devices in a mesh: space: 8 (over z, x), blk: 4 (over y, core).
Axes of the slice: x: 2, y: 2, z: 4, core: 2. Of those that a mesh axis runs over, the one named last changes fastest.
Arguments:
- pressure: float32 [512, 16384], P('blk', 'space'), may hold values from -6 to 6
- final_steps: float32 [128, 16384], P(None, 'space'), may hold values from -6 to 6
- weights: float32 [16384], P('space'), may hold values from 0.5 to 4.5, as said below
Outputs:
- spectra: bfloat16 [4, 128, 2, 16384], P(None, 'blk', None, 'space')
- csd: float32 [2, 128, 4, 4], P(None, 'blk')
The draws below stay inside these ranges and needn't reach their ends.
Inputs may be any that keep to these rules, and one draw needn't show every extreme that they name: Positive weights.
All inputs are finite; a program needn't handle non-finite values.
Results may differ from the reference program's by a relative error of at most 0.0055.
Values may be sent and summed in bfloat16 or wider, within the bound.
A program may use at most 64 MiB of HBM per device.

```python
import math
import jax
import jax.numpy as jnp
from jax import lax

HOP = 128
BLEN = 256
NFREQ = 128
BLOCKS = 4
NPTS = 16384


def draw_weights(key, part):
    key = jax.random.fold_in(key, 7)
    ramp = 1.0 + 2.0 * jnp.arange(NPTS, dtype=jnp.float32) / NPTS
    spread = jax.random.uniform(key, (NPTS,), jnp.float32, 0.5, 1.5)
    return ramp * spread


def levels(own_key, dims, shards, least, top_value):
    level, own = 1.0, jax.random.fold_in(own_key, 6)
    for axis_at, shards_of in shards:
        heights = jnp.exp(jax.random.uniform(jax.random.fold_in(own, axis_at), (shards_of,), jnp.float32, least / len(shards), top_value / len(shards)))
        level = level * jnp.repeat(heights, dims[axis_at] // shards_of).reshape([-1 if axis == axis_at else 1 for axis in range(len(dims))])
    return level


def noise(own_key, shape, scale, most, split=(), kind=jnp.bfloat16):
    factor_of = levels(own_key, shape, split, -0.22, 0.18) if split else 1.0
    values = jax.random.normal(own_key, shape, jnp.float32) * scale * factor_of
    return jnp.minimum(jnp.maximum(values, -most), most).astype(kind)


def setup_inputs(seed: int = 0) -> dict:
    keys = jax.random.split(jax.random.key(seed), 4)
    return {
        "pressure": noise(keys[0], (BLOCKS * HOP, NPTS), 1.0, 6.0, ((0, 4), (1, 8)), jnp.float32),
        "final_steps": noise(keys[1], (HOP, NPTS), 1.0, 6.0, ((1, 8),), jnp.float32),
        "weights": draw_weights(jax.random.fold_in(keys[3], 71), 0),
    }


def make_table(blen, nfreq):
    t = jnp.arange(blen, dtype=jnp.int32)
    k = jnp.arange(nfreq, dtype=jnp.int32)
    phase = k[:, None] * t[None, :] % blen
    angle = 2.0 * math.pi / blen * phase.astype(jnp.float32)
    scale = 1.0 / math.sqrt(3.0 * blen / 8.0)
    table = jnp.stack([jnp.cos(angle) * scale, -jnp.sin(angle) * scale], axis=1)
    return table.reshape(2 * nfreq, blen).astype(jnp.bfloat16)

def make_hann(blen):
    t = jnp.arange(blen, dtype=jnp.float32)
    return 0.5 - 0.5 * jnp.cos(2.0 * math.pi / blen * t)

def cross_sums(spectra, weights, count):
    values = spectra.astype(jnp.float32)
    real_part = values[:, :, 0]
    imag_part = values[:, :, 1]
    high = lax.Precision.HIGHEST
    real_w = real_part * weights
    imag_w = imag_part * weights
    first = jnp.einsum('ikn,jkn->kij', real_w, real_part, precision=high) + jnp.einsum('ikn,jkn->kij', imag_w, imag_part, precision=high)
    second = jnp.einsum('ikn,jkn->kij', imag_w, real_part, precision=high) - jnp.einsum('ikn,jkn->kij', real_w, imag_part, precision=high)
    return jnp.stack([first, second], axis=0) / count

def reference(pressure, final_steps, weights):
    total = lax.optimization_barrier(jnp.sum(pressure, axis=0)) + lax.optimization_barrier(jnp.sum(final_steps, axis=0))
    mean = total / (HOP * (BLOCKS + 1))
    full = jnp.concatenate([pressure, final_steps], axis=0) - mean
    table = make_table(BLEN, NFREQ)
    hann = make_hann(BLEN)
    blocks = []
    for index in range(BLOCKS):
        piece = full[index * HOP:index * HOP + BLEN]
        windowed = (piece * hann[:, None]).astype(jnp.bfloat16)
        coeff = jnp.dot(table, windowed, preferred_element_type=jnp.float32).astype(jnp.bfloat16)
        blocks.append(coeff.reshape(NFREQ, 2, NPTS))
    spectra = jnp.stack(blocks, axis=0)
    csd = cross_sums(spectra, weights, float(NPTS))
    return (spectra, csd)
```

```python
import functools
import math

import jax
import jax.numpy as jnp
import ml_dtypes
import numpy as np
from jax import lax
from jax.experimental import pallas as pl
from jax.experimental.pallas import tpu as pltpu
from jax.sharding import PartitionSpec as P

HOP = 128
LANES = 128
CHUNKS = 8
MESH = pl.DeviceIdType.MESH


def make_tables(blen, nfreq, groups):
    t = np.arange(blen)
    k = np.arange(nfreq)
    angle = 2.0 * math.pi / blen * (k[:, None] * t[None, :] % blen)
    scale = 1.0 / math.sqrt(3.0 * blen / 8.0)
    table = np.stack([np.cos(angle) * scale, -np.sin(angle) * scale], axis=1)
    table = table.astype(ml_dtypes.bfloat16).astype(np.float64)
    hann = 0.5 - 0.5 * np.cos(2.0 * math.pi / blen * t)
    table = (table * hann).reshape(groups, nfreq // groups, 2, blen)
    split = table.transpose(0, 2, 1, 3).reshape(groups, -1, blen)
    mixed = table.reshape(groups, -1, blen)
    return np.concatenate([split, mixed], axis=1).astype(ml_dtypes.bfloat16)


def each(first, last, body):
    if last - first <= 8:
        for index in range(first, last):
            body(index)
    else:
        pl.loop(first, last)(body)


PAIRS = [(i, j) for i in range(4) for j in range(i, 4)]
CROSS = [(i, j) for i in range(4) for j in range(i + 1, 4)]


def kernel(
    n_space, n_blk, count,
    p_ref, f_ref, w_ref, t_ref, spec_ref, csd_ref,
    p_buf, f_buf, w_buf, t_buf, ranges, sums, x, acc, rows,
    p_sem, f_sem, w_sem, t_sem,
    across_send, across_recv, core_send, core_recv, relay_send, relay_recv,
    sum_send, sum_recv, csd_send, csd_recv,
):
    s, q = lax.axis_index("space"), lax.axis_index("blk")
    width = p_buf.shape[2]
    half = t_buf.shape[0] // 2
    freqs = half // 2
    beside = q + 1 - 2 * (q % 2)
    across = (q + 2) % 4
    diagonal = beside + 2 - 4 * (beside // 2)

    def columns(c):
        return pl.ds(pl.multiple_of(c * width, width), width)

    def load(source, target, sem, c):
        return pltpu.make_async_copy(source.at[:, columns(c)], target.at[c], sem.at[c])

    table_copy = pltpu.make_async_copy(t_ref.at[q], t_buf, t_sem)
    weight_copy = pltpu.make_async_copy(w_ref, w_buf, w_sem)

    barrier = pltpu.get_barrier_semaphore()
    for other in (across, beside, diagonal):
        pl.semaphore_signal(barrier, inc=1, device_id=(s, other), device_id_type=MESH)

    def greet(offset):
        pl.semaphore_signal(barrier, inc=1, device_id=((s + offset) % n_space, q), device_id_type=MESH)

    each(1, n_space, greet)

    for c in range(CHUNKS):
        load(p_ref, p_buf, p_sem, c).start()
    table_copy.start()
    weight_copy.start()
    for c in range(CHUNKS):
        load(f_ref, f_buf, f_sem, c).start()

    def centre(source, target, c, slot):
        values = source[c]
        total = jnp.sum(values, axis=0, keepdims=True)
        sums[slot, :, columns(c)] = total
        target[...] = (values - total * (1.0 / HOP)).astype(jnp.bfloat16)

    @pl.loop(0, CHUNKS)
    def _(c):
        load(p_ref, p_buf, p_sem, c).wait()
        centre(p_buf, ranges.at[c, q], c, q)

    pl.semaphore_wait(barrier, 3 + n_space - 1)

    def send(ref, index, send_sem, recv_sem, other):
        return pltpu.make_async_remote_copy(
            src_ref=ref.at[index], dst_ref=ref.at[index], send_sem=send_sem, recv_sem=recv_sem,
            device_id=(s, other), device_id_type=MESH,
        )

    def sum_copy(which, owner):
        return send(sums, owner, sum_send.at[which], sum_recv.at[which], (across, beside, diagonal)[which])

    def across_copy(c, owner):
        return send(ranges, (c, owner), across_send.at[c], across_recv.at[c], across)

    def core_copy(c, owner):
        return send(ranges, (c, owner), core_send.at[c], core_recv.at[c], beside)

    def relay_copy(c, owner):
        return send(ranges, (c, owner), relay_send.at[c], relay_recv.at[c], beside)

    for which in range(3):
        sum_copy(which, q).start()
    for c in range(CHUNKS):
        across_copy(c, q).start()
    for c in range(CHUNKS):
        core_copy(c, q).start()

    @pl.loop(0, CHUNKS)
    def _(c):
        load(f_ref, f_buf, f_sem, c).wait()
        centre(f_buf, ranges.at[c, n_blk], c, n_blk)

    acc[...] = jnp.zeros_like(acc)
    table_copy.wait()
    weight_copy.wait()
    for which, owner in enumerate((across, beside, diagonal)):
        sum_copy(which, owner).wait_recv()

    def coefficients(c, row):
        table = t_buf[row:row + half, :]
        wide = table.astype(jnp.float32)
        first = jnp.sum(wide[:, :HOP], axis=1, keepdims=True)
        second = jnp.sum(wide[:, HOP:], axis=1, keepdims=True)
        parts = [sums[r, :, columns(c)] for r in range(n_blk + 1)]
        mean = sum(parts[1:], parts[0]) * (1.0 / (HOP * (n_blk + 1)))
        offsets = [part * (1.0 / HOP) - mean for part in parts]
        for b in range(n_blk):
            pair = ranges[c, b:b + 2].reshape(2 * HOP, width)
            value = jnp.dot(table, pair, preferred_element_type=jnp.float32)
            yield b, (value + (first * offsets[b] + second * offsets[b + 1])).astype(jnp.bfloat16)

    def accumulate(c):
        for b, value in coefficients(c, 0):
            x[b] = value.astype(jnp.float32)
        for g in range(freqs // 8):
            low, high = slice(8 * g, 8 * g + 8), slice(freqs + 8 * g, freqs + 8 * g + 8)
            totals = [acc[m, low, :] for m in range(len(PAIRS) + len(CROSS))]
            for tile in range(width // LANES):
                lanes = slice(tile * LANES, (tile + 1) * LANES)
                weight = w_buf[:, pl.ds(pl.multiple_of(c * width + tile * LANES, LANES), LANES)]
                re = [x[b, low, lanes] for b in range(n_blk)]
                im = [x[b, high, lanes] for b in range(n_blk)]
                re_w = [value * weight for value in re]
                im_w = [value * weight for value in im]
                for m, (i, j) in enumerate(PAIRS):
                    totals[m] += re_w[i] * re[j] + im_w[i] * im[j]
                for m, (i, j) in enumerate(CROSS):
                    totals[len(PAIRS) + m] += im_w[i] * re[j] - re_w[i] * im[j]
            for m, total in enumerate(totals):
                acc[m, low, :] = total

    def write(c):
        for b, value in coefficients(c, half):
            spec_ref[b, :, columns(c)] = value

    @pl.loop(0, CHUNKS + 1)
    def _(c):
        @pl.when(c < CHUNKS)
        def _():
            across_copy(c, across).wait_recv()
            relay_copy(c, across).start()

        @pl.when(c > 0)
        def _():
            core_copy(c - 1, beside).wait_recv()
            relay_copy(c - 1, diagonal).wait_recv()
            accumulate(c - 1)

        @pl.when((c > 0) & (c < CHUNKS))
        def _():
            write(c - 1)

    flat = acc[...].reshape(-1, LANES)
    rows[s] = jnp.sum(flat.T, axis=0, keepdims=True)

    def row_copy(offset, owner, peer):
        return pltpu.make_async_remote_copy(
            src_ref=rows.at[owner], dst_ref=rows.at[owner],
            send_sem=csd_send.at[offset], recv_sem=csd_recv.at[owner],
            device_id=(peer, q), device_id_type=MESH,
        )

    each(1, n_space, lambda offset: row_copy(offset, s, (s + offset) % n_space).start())
    write(CHUNKS - 1)

    def arrived(offset):
        peer = (s + offset) % n_space
        row_copy(offset, peer, peer).wait_recv()

    each(1, n_space, arrived)
    csd_ref[...] = jnp.sum(rows[...], axis=0) * (1.0 / count)

    for which in range(3):
        sum_copy(which, q).wait_send()
    for c in range(CHUNKS):
        across_copy(c, q).wait_send()
        core_copy(c, q).wait_send()
        relay_copy(c, across).wait_send()
    each(1, n_space, lambda offset: row_copy(offset, s, (s + offset) % n_space).wait_send())


def local(n_space, n_blk, pressure, final_steps, weights, tables):
    points = pressure.shape[1]
    width = points // CHUNKS
    half = tables.shape[1] // 2
    freqs = half // 2
    kinds = len(PAIRS) + len(CROSS)
    dma = pltpu.SemaphoreType.DMA
    any_space = pl.BlockSpec(memory_space=pl.ANY)
    in_vmem = pl.BlockSpec(memory_space=pltpu.VMEM)
    spectra, row = pl.pallas_call(
        functools.partial(kernel, n_space, n_blk, float(points * n_space)),
        out_shape=(
            jax.ShapeDtypeStruct((n_blk, half, points), jnp.bfloat16),
            jax.ShapeDtypeStruct((1, kinds * freqs), jnp.float32),
        ),
        in_specs=[any_space] * 4,
        out_specs=(in_vmem, in_vmem),
        scratch_shapes=[
            pltpu.VMEM((CHUNKS, HOP, width), jnp.float32),
            pltpu.VMEM((CHUNKS, HOP, width), jnp.float32),
            pltpu.VMEM((1, points), jnp.float32),
            pltpu.VMEM(tables.shape[1:], jnp.bfloat16),
            pltpu.VMEM((CHUNKS, n_blk + 1, HOP, width), jnp.bfloat16),
            pltpu.VMEM((n_blk + 1, 1, points), jnp.float32),
            pltpu.VMEM((n_blk, half, width), jnp.float32),
            pltpu.VMEM((kinds, freqs, LANES), jnp.float32),
            pltpu.VMEM((n_space, 1, kinds * freqs), jnp.float32),
            dma((CHUNKS,)), dma((CHUNKS,)), dma(()), dma(()),
            dma((CHUNKS,)), dma((CHUNKS,)), dma((CHUNKS,)), dma((CHUNKS,)), dma((CHUNKS,)), dma((CHUNKS,)),
            dma((3,)), dma((3,)), dma((n_space,)), dma((n_space,)),
        ],
        compiler_params=pltpu.CompilerParams(
            collective_id=0, has_side_effects=True, vmem_limit_bytes=32 * 1024 * 1024
        ),
    )(pressure, final_steps, weights.reshape(1, points), tables)
    spectra = spectra.reshape(n_blk, freqs, 2, points)
    row = row.reshape(kinds, freqs)
    zero = jnp.zeros_like(row[0])
    full = []
    for i in range(4):
        for j in range(4):
            full.append(row[PAIRS.index((min(i, j), max(i, j)))])
    for i in range(4):
        for j in range(4):
            at = len(PAIRS) + CROSS.index((min(i, j), max(i, j))) if i != j else 0
            full.append(zero if i == j else row[at] if i < j else -row[at])
    csd = jnp.stack(full).reshape(2, 4, 4, freqs).transpose(0, 3, 1, 2)
    return spectra, csd


def solution(mesh):
    n_space, n_blk = mesh.shape["space"], mesh.shape["blk"]
    tables = make_tables(2 * HOP, HOP, n_blk)
    mapped = jax.shard_map(
        functools.partial(local, n_space, n_blk),
        mesh=mesh,
        in_specs=(P("blk", "space"), P(None, "space"), P("space"), P()),
        out_specs=(P(None, "blk", None, "space"), P(None, "blk", None, None)),
        check_vma=False,
    )

    def run(pressure, final_steps, weights):
        return mapped(pressure, final_steps, weights, jnp.asarray(tables))

    return run
```

```python
import functools
import math

import jax
import jax.numpy as jnp
import ml_dtypes
import numpy as np
from jax import lax
from jax.experimental import pallas as pl
from jax.experimental.pallas import tpu as pltpu
from jax.sharding import PartitionSpec as P

HOP = 128
LANES = 128
CHUNKS = 8
MESH = pl.DeviceIdType.MESH


def make_tables(blen, nfreq, groups):
    t = np.arange(blen)
    k = np.arange(nfreq)
    angle = 2.0 * math.pi / blen * (k[:, None] * t[None, :] % blen)
    scale = 1.0 / math.sqrt(3.0 * blen / 8.0)
    table = np.stack([np.cos(angle) * scale, -np.sin(angle) * scale], axis=1)
    table = table.astype(ml_dtypes.bfloat16).astype(np.float64)
    hann = 0.5 - 0.5 * np.cos(2.0 * math.pi / blen * t)
    table = (table * hann).reshape(groups, nfreq // groups, 2, blen)
    split = table.transpose(0, 2, 1, 3).reshape(groups, -1, blen)
    mixed = table.reshape(groups, -1, blen)
    return np.concatenate([split, mixed], axis=1).astype(ml_dtypes.bfloat16)


def each(first, last, body):
    if last - first <= 8:
        for index in range(first, last):
            body(index)
    else:
        pl.loop(first, last)(body)


PAIRS = [(i, j) for i in range(4) for j in range(i, 4)]
CROSS = [(i, j) for i in range(4) for j in range(i + 1, 4)]


def kernel(
    n_space, n_blk, count,
    p_ref, f_ref, w_ref, t_ref, spec_ref, csd_ref,
    p_buf, f_buf, w_buf, t_buf, ranges, sums, x, acc, rows,
    p_sem, f_sem, w_sem, t_sem,
    across_send, across_recv, core_send, core_recv, relay_send, relay_recv,
    sum_send, sum_recv, csd_send, csd_recv,
):
    s, q = lax.axis_index("space"), lax.axis_index("blk")
    width = p_buf.shape[2]
    half = t_buf.shape[0] // 2
    freqs = half // 2
    beside = q + 1 - 2 * (q % 2)
    across = (q + 2) % 4
    diagonal = beside + 2 - 4 * (beside // 2)

    def columns(c):
        return pl.ds(pl.multiple_of(c * width, width), width)

    def load(source, target, sem, c):
        return pltpu.make_async_copy(source.at[:, columns(c)], target.at[c], sem.at[c])

    table_copy = pltpu.make_async_copy(t_ref.at[q], t_buf, t_sem)
    weight_copy = pltpu.make_async_copy(w_ref, w_buf, w_sem)

    barrier = pltpu.get_barrier_semaphore()
    for other in (across, beside, diagonal):
        pl.semaphore_signal(barrier, inc=1, device_id=(s, other), device_id_type=MESH)

    def greet(offset):
        pl.semaphore_signal(barrier, inc=1, device_id=((s + offset) % n_space, q), device_id_type=MESH)

    each(1, n_space, greet)

    for c in range(CHUNKS):
        load(p_ref, p_buf, p_sem, c).start()
    table_copy.start()
    weight_copy.start()
    for c in range(CHUNKS):
        load(f_ref, f_buf, f_sem, c).start()

    def centre(source, target, c, slot):
        values = source[c]
        total = jnp.sum(values, axis=0, keepdims=True)
        sums[slot, :, columns(c)] = total
        target[...] = (values - total * (1.0 / HOP)).astype(jnp.bfloat16)

    def send(ref, index, send_sem, recv_sem, other):
        return pltpu.make_async_remote_copy(
            src_ref=ref.at[index], dst_ref=ref.at[index], send_sem=send_sem, recv_sem=recv_sem,
            device_id=(s, other), device_id_type=MESH,
        )

    def sum_copy(which, owner):
        return send(sums, owner, sum_send.at[which], sum_recv.at[which], (across, beside, diagonal)[which])

    def across_copy(c, owner):
        return send(ranges, (c, owner), across_send.at[c], across_recv.at[c], across)

    def core_copy(c, owner):
        return send(ranges, (c, owner), core_send.at[c], core_recv.at[c], beside)

    def relay_copy(c, owner):
        return send(ranges, (c, owner), relay_send.at[c], relay_recv.at[c], beside)

    def prepare(c):
        load(p_ref, p_buf, p_sem, c).wait()
        centre(p_buf, ranges.at[c, q], c, q)

    def share(c):
        across_copy(c, q).start()
        core_copy(c, q).start()

    prepare(0)
    pl.semaphore_wait(barrier, 3 + n_space - 1)
    share(0)
    prepare(1)
    share(1)
    pl.loop(2, CHUNKS)(prepare)
    for which in range(3):
        sum_copy(which, q).start()
    for c in range(2, CHUNKS):
        share(c)

    @pl.loop(0, CHUNKS)
    def _(c):
        load(f_ref, f_buf, f_sem, c).wait()
        centre(f_buf, ranges.at[c, n_blk], c, n_blk)

    acc[...] = jnp.zeros_like(acc)
    table_copy.wait()
    weight_copy.wait()
    for which, owner in enumerate((across, beside, diagonal)):
        sum_copy(which, owner).wait_recv()

    def coefficients(c, row):
        table = t_buf[row:row + half, :]
        wide = table.astype(jnp.float32)
        first = jnp.sum(wide[:, :HOP], axis=1, keepdims=True)
        second = jnp.sum(wide[:, HOP:], axis=1, keepdims=True)
        parts = [sums[r, :, columns(c)] for r in range(n_blk + 1)]
        mean = sum(parts[1:], parts[0]) * (1.0 / (HOP * (n_blk + 1)))
        offsets = [part * (1.0 / HOP) - mean for part in parts]
        for b in range(n_blk):
            pair = ranges[c, b:b + 2].reshape(2 * HOP, width)
            value = jnp.dot(table, pair, preferred_element_type=jnp.float32)
            yield b, (value + (first * offsets[b] + second * offsets[b + 1])).astype(jnp.bfloat16)

    def accumulate(c):
        for b, value in coefficients(c, 0):
            x[b] = value.astype(jnp.float32)
        for g in range(freqs // 8):
            low, high = slice(8 * g, 8 * g + 8), slice(freqs + 8 * g, freqs + 8 * g + 8)
            totals = [acc[m, low, :] for m in range(len(PAIRS) + len(CROSS))]
            for tile in range(width // LANES):
                lanes = slice(tile * LANES, (tile + 1) * LANES)
                weight = w_buf[:, pl.ds(pl.multiple_of(c * width + tile * LANES, LANES), LANES)]
                re = [x[b, low, lanes] for b in range(n_blk)]
                im = [x[b, high, lanes] for b in range(n_blk)]
                re_w = [value * weight for value in re]
                im_w = [value * weight for value in im]
                for m, (i, j) in enumerate(PAIRS):
                    totals[m] += re_w[i] * re[j] + im_w[i] * im[j]
                for m, (i, j) in enumerate(CROSS):
                    totals[len(PAIRS) + m] += im_w[i] * re[j] - re_w[i] * im[j]
            for m, total in enumerate(totals):
                acc[m, low, :] = total

    def write(c):
        for b, value in coefficients(c, half):
            spec_ref[b, :, :, columns(c)] = value.reshape(freqs, 2, width)

    @pl.loop(0, CHUNKS + 1)
    def _(c):
        @pl.when(c < CHUNKS)
        def _():
            across_copy(c, across).wait_recv()
            relay_copy(c, across).start()

        @pl.when(c > 0)
        def _():
            core_copy(c - 1, beside).wait_recv()
            relay_copy(c - 1, diagonal).wait_recv()
            accumulate(c - 1)

        @pl.when((c > 0) & (c < CHUNKS))
        def _():
            write(c - 1)

    flat = acc[...].reshape(-1, LANES)
    rows[s] = jnp.sum(flat.T, axis=0, keepdims=True)

    def row_copy(offset, owner, peer):
        return pltpu.make_async_remote_copy(
            src_ref=rows.at[owner], dst_ref=rows.at[owner],
            send_sem=csd_send.at[offset], recv_sem=csd_recv.at[owner],
            device_id=(peer, q), device_id_type=MESH,
        )

    each(1, n_space, lambda offset: row_copy(offset, s, (s + offset) % n_space).start())
    write(CHUNKS - 1)

    def arrived(offset):
        peer = (s + offset) % n_space
        row_copy(offset, peer, peer).wait_recv()

    each(1, n_space, arrived)
    total = jnp.sum(rows[...], axis=0) * (1.0 / count)
    csd_ref[...] = jnp.zeros_like(csd_ref)
    for m, (i, j) in enumerate(PAIRS + CROSS):
        line = total[:, m * freqs:(m + 1) * freqs]
        if m < len(PAIRS):
            for row in {4 * i + j, 4 * j + i}:
                csd_ref[row:row + 1, :] = line
        else:
            csd_ref[16 + 4 * i + j:17 + 4 * i + j, :] = line
            csd_ref[16 + 4 * j + i:17 + 4 * j + i, :] = -line

    for which in range(3):
        sum_copy(which, q).wait_send()
    for c in range(CHUNKS):
        across_copy(c, q).wait_send()
        core_copy(c, q).wait_send()
        relay_copy(c, across).wait_send()
    each(1, n_space, lambda offset: row_copy(offset, s, (s + offset) % n_space).wait_send())


def local(n_space, n_blk, pressure, final_steps, weights, tables):
    points = pressure.shape[1]
    width = points // CHUNKS
    half = tables.shape[1] // 2
    freqs = half // 2
    kinds = len(PAIRS) + len(CROSS)
    dma = pltpu.SemaphoreType.DMA
    in_hbm = pl.BlockSpec(memory_space=pltpu.HBM)
    in_vmem = pl.BlockSpec(memory_space=pltpu.VMEM)
    spectra, csd = pl.pallas_call(
        functools.partial(kernel, n_space, n_blk, float(points * n_space)),
        out_shape=(
            jax.ShapeDtypeStruct((n_blk, freqs, 2, points), jnp.bfloat16),
            jax.ShapeDtypeStruct((32, freqs), jnp.float32),
        ),
        in_specs=[in_hbm] * 4,
        out_specs=(in_vmem, in_vmem),
        scratch_shapes=[
            pltpu.VMEM((CHUNKS, HOP, width), jnp.float32),
            pltpu.VMEM((CHUNKS, HOP, width), jnp.float32),
            pltpu.VMEM((1, points), jnp.float32),
            pltpu.VMEM(tables.shape[1:], jnp.bfloat16),
            pltpu.VMEM((CHUNKS, n_blk + 1, HOP, width), jnp.bfloat16),
            pltpu.VMEM((n_blk + 1, 1, points), jnp.float32),
            pltpu.VMEM((n_blk, half, width), jnp.float32),
            pltpu.VMEM((kinds, freqs, LANES), jnp.float32),
            pltpu.VMEM((n_space, 1, kinds * freqs), jnp.float32),
            dma((CHUNKS,)), dma((CHUNKS,)), dma(()), dma(()),
            dma((CHUNKS,)), dma((CHUNKS,)), dma((CHUNKS,)), dma((CHUNKS,)), dma((CHUNKS,)), dma((CHUNKS,)),
            dma((3,)), dma((3,)), dma((n_space,)), dma((n_space,)),
        ],
        compiler_params=pltpu.CompilerParams(
            collective_id=0, has_side_effects=True, vmem_limit_bytes=52 * 1024 * 1024
        ),
    )(pressure, final_steps, weights.reshape(1, points), tables)
    csd = csd.reshape(2, 4, 4, freqs).transpose(0, 3, 1, 2)
    return spectra, csd


def solution(mesh):
    n_space, n_blk = mesh.shape["space"], mesh.shape["blk"]
    tables = make_tables(2 * HOP, HOP, n_blk)
    mapped = jax.shard_map(
        functools.partial(local, n_space, n_blk),
        mesh=mesh,
        in_specs=(P("blk", "space"), P(None, "space"), P("space"), P()),
        out_specs=(P(None, "blk", None, "space"), P(None, "blk", None, None)),
        check_vma=False,
    )

    def run(pressure, final_steps, weights):
        return mapped(pressure, final_steps, weights, jnp.asarray(tables))

    return run
```

```python
import functools
import math

import jax
import jax.numpy as jnp
from jax import lax
from jax.experimental import pallas as pl
from jax.experimental.pallas import tpu as pltpu
from jax.sharding import PartitionSpec as P

HOP = 128
LANES = 128
CHUNKS = 8
MESH = pl.DeviceIdType.MESH


def make_table(rows, freqs, group):
    blen = 2 * HOP
    row = lax.broadcasted_iota(jnp.int32, (rows, blen), 0)
    t = lax.broadcasted_iota(jnp.int32, (rows, blen), 1)
    mixed = row >= 2 * freqs
    inner = jnp.where(mixed, row - 2 * freqs, row)
    k = group * freqs + jnp.where(mixed, lax.div(inner, 2), lax.rem(inner, freqs))
    part = jnp.where(mixed, lax.rem(inner, 2), lax.div(inner, freqs))
    step = 2.0 * math.pi / blen
    phase = lax.rem(k * t + part * (blen // 4), blen)
    table = jnp.cos(phase.astype(jnp.float32) * step) * (1.0 / math.sqrt(3.0 * blen / 8.0))
    hann = 0.5 - 0.5 * jnp.cos(t[:8].astype(jnp.float32) * step)
    return table.astype(jnp.bfloat16).astype(jnp.float32) * hann[:1]


def each(first, last, body):
    if last - first <= 8:
        for index in range(first, last):
            body(index)
    else:
        pl.loop(first, last)(body)


PAIRS = [(i, j) for i in range(4) for j in range(i, 4)]
CROSS = [(i, j) for i in range(4) for j in range(i + 1, 4)]


def kernel(
    n_space, n_blk, count,
    p_ref, f_ref, w_ref, spec_ref, csd_ref,
    p_buf, f_buf, w_buf, t_buf, edges, ranges, sums, x, acc, rows,
    p_sem, f_sem, w_sem,
    across_send, across_recv, core_send, core_recv, relay_send, relay_recv,
    sum_send, sum_recv, csd_send, csd_recv,
):
    s, q = lax.axis_index("space"), lax.axis_index("blk")
    width = p_buf.shape[2]
    half = t_buf.shape[0] // 2
    freqs = half // 2
    beside = q + 1 - 2 * (q % 2)
    across = (q + 2) % 4
    diagonal = beside + 2 - 4 * (beside // 2)

    def columns(c):
        return pl.ds(pl.multiple_of(c * width, width), width)

    def load(source, target, sem, c):
        return pltpu.make_async_copy(source.at[:, columns(c)], target.at[c], sem.at[c])

    weight_copy = pltpu.make_async_copy(w_ref, w_buf, w_sem)

    barrier = pltpu.get_barrier_semaphore()
    for other in (across, beside, diagonal):
        pl.semaphore_signal(barrier, inc=1, device_id=(s, other), device_id_type=MESH)

    def greet(offset):
        pl.semaphore_signal(barrier, inc=1, device_id=((s + offset) % n_space, q), device_id_type=MESH)

    each(1, n_space, greet)

    for c in range(CHUNKS):
        load(p_ref, p_buf, p_sem, c).start()
    weight_copy.start()
    for c in range(CHUNKS):
        load(f_ref, f_buf, f_sem, c).start()

    def centre(source, target, c, slot):
        values = source[c]
        total = jnp.sum(values, axis=0, keepdims=True)
        sums[slot, :, columns(c)] = total
        target[...] = (values - total * (1.0 / HOP)).astype(jnp.bfloat16)

    def send(ref, index, send_sem, recv_sem, other):
        return pltpu.make_async_remote_copy(
            src_ref=ref.at[index], dst_ref=ref.at[index], send_sem=send_sem, recv_sem=recv_sem,
            device_id=(s, other), device_id_type=MESH,
        )

    def sum_copy(which, owner):
        return send(sums, owner, sum_send.at[which], sum_recv.at[which], (across, beside, diagonal)[which])

    def across_copy(c, owner):
        return send(ranges, (c, owner), across_send.at[c], across_recv.at[c], across)

    def core_copy(c, owner):
        return send(ranges, (c, owner), core_send.at[c], core_recv.at[c], beside)

    def relay_copy(c, owner):
        return send(ranges, (c, owner), relay_send.at[c], relay_recv.at[c], beside)

    def prepare(c):
        load(p_ref, p_buf, p_sem, c).wait()
        centre(p_buf, ranges.at[c, q], c, q)

    def share(c):
        across_copy(c, q).start()
        core_copy(c, q).start()

    prepare(0)
    pl.semaphore_wait(barrier, 3 + n_space - 1)
    share(0)
    prepare(1)
    share(1)
    pl.loop(2, CHUNKS)(prepare)
    for which in range(3):
        sum_copy(which, q).start()
    for c in range(2, CHUNKS):
        share(c)

    @pl.loop(0, CHUNKS)
    def _(c):
        load(f_ref, f_buf, f_sem, c).wait()
        centre(f_buf, ranges.at[c, n_blk], c, n_blk)

    acc[...] = jnp.zeros_like(acc)
    table = make_table(2 * half, freqs, q)
    t_buf[...] = table.astype(jnp.bfloat16)
    for side in range(2):
        total = jnp.sum(table[:, side * HOP:(side + 1) * HOP], axis=1, keepdims=True)
        edges[side] = jnp.broadcast_to(total, edges.shape[1:])
    weight_copy.wait()
    for which, owner in enumerate((across, beside, diagonal)):
        sum_copy(which, owner).wait_recv()

    def coefficients(c, first, last):
        before, after = (jnp.tile(edges[side, first:last, :], (1, width // LANES)) for side in range(2))
        parts = [sums[r, :, columns(c)] for r in range(n_blk + 1)]
        mean = sum(parts[1:], parts[0]) * (1.0 / (HOP * (n_blk + 1)))
        offsets = [part * (1.0 / HOP) - mean for part in parts]
        for b in range(n_blk):
            pair = ranges[c, b:b + 2].reshape(2 * HOP, width)
            value = jnp.dot(t_buf[first:last, :], pair, preferred_element_type=jnp.float32)
            yield b, (value + (before * offsets[b] + after * offsets[b + 1])).astype(jnp.bfloat16)

    def keep(b, value):
        x[b] = value.astype(jnp.float32)

    def write(c, b, value):
        spec_ref[b, :, :, columns(c)] = value.reshape(freqs, 2, width)

    def accumulate(c):
        for g in range(freqs // 8):
            low, high = slice(8 * g, 8 * g + 8), slice(freqs + 8 * g, freqs + 8 * g + 8)
            totals = [acc[m, low, :] for m in range(len(PAIRS) + len(CROSS))]
            for tile in range(width // LANES):
                lanes = slice(tile * LANES, (tile + 1) * LANES)
                weight = w_buf[:, pl.ds(pl.multiple_of(c * width + tile * LANES, LANES), LANES)]
                re = [x[b, low, lanes] for b in range(n_blk)]
                im = [x[b, high, lanes] for b in range(n_blk)]
                re_w = [value * weight for value in re]
                im_w = [value * weight for value in im]
                for m, (i, j) in enumerate(PAIRS):
                    totals[m] += re_w[i] * re[j] + im_w[i] * im[j]
                for m, (i, j) in enumerate(CROSS):
                    totals[len(PAIRS) + m] += im_w[i] * re[j] - re_w[i] * im[j]
            for m, total in enumerate(totals):
                acc[m, low, :] = total

    def receive(c):
        across_copy(c, across).wait_recv()
        relay_copy(c, across).start()

    def receive_relayed(c):
        core_copy(c, beside).wait_recv()
        relay_copy(c, diagonal).wait_recv()

    receive(0)

    @pl.loop(1, CHUNKS)
    def _(c):
        receive(c)
        receive_relayed(c - 1)
        for b, value in coefficients(c - 1, 0, 2 * half):
            keep(b, value[:half])
            write(c - 1, b, value[half:])
        accumulate(c - 1)

    receive_relayed(CHUNKS - 1)
    for b, value in coefficients(CHUNKS - 1, 0, half):
        keep(b, value)
    accumulate(CHUNKS - 1)

    flat = acc[...].reshape(-1, LANES)
    rows[s] = jnp.sum(flat.T, axis=0, keepdims=True)

    def row_copy(offset, owner, peer):
        return pltpu.make_async_remote_copy(
            src_ref=rows.at[owner], dst_ref=rows.at[owner],
            send_sem=csd_send.at[offset], recv_sem=csd_recv.at[owner],
            device_id=(peer, q), device_id_type=MESH,
        )

    each(1, n_space, lambda offset: row_copy(offset, s, (s + offset) % n_space).start())
    for b, value in coefficients(CHUNKS - 1, half, 2 * half):
        write(CHUNKS - 1, b, value)

    def arrived(offset):
        peer = (s + offset) % n_space
        row_copy(offset, peer, peer).wait_recv()

    each(1, n_space, arrived)
    total = jnp.sum(rows[...], axis=0) * (1.0 / count)
    csd_ref[...] = jnp.zeros_like(csd_ref)
    for m, (i, j) in enumerate(PAIRS + CROSS):
        line = total[:, m * freqs:(m + 1) * freqs]
        if m < len(PAIRS):
            for row in {4 * i + j, 4 * j + i}:
                csd_ref[row:row + 1, :] = line
        else:
            csd_ref[16 + 4 * i + j:17 + 4 * i + j, :] = line
            csd_ref[16 + 4 * j + i:17 + 4 * j + i, :] = -line

    for which in range(3):
        sum_copy(which, q).wait_send()
    for c in range(CHUNKS):
        across_copy(c, q).wait_send()
        core_copy(c, q).wait_send()
        relay_copy(c, across).wait_send()
    each(1, n_space, lambda offset: row_copy(offset, s, (s + offset) % n_space).wait_send())


def finish(spec_ref, csd_ref, spec_out, csd_out, sems):
    copies = [
        pltpu.make_async_copy(spec_ref, spec_out, sems.at[0]),
        pltpu.make_async_copy(csd_ref, csd_out, sems.at[1]),
    ]
    for copy in copies:
        copy.start()
    for copy in copies:
        copy.wait()


def local(n_space, n_blk, pressure, final_steps, weights):
    points = pressure.shape[1]
    width = points // CHUNKS
    freqs = HOP // n_blk
    half = 2 * freqs
    kinds = len(PAIRS) + len(CROSS)
    dma = pltpu.SemaphoreType.DMA
    in_hbm = pl.BlockSpec(memory_space=pltpu.HBM)
    in_vmem = pl.BlockSpec(memory_space=pltpu.VMEM)
    spectra, csd = pl.pallas_call(
        functools.partial(kernel, n_space, n_blk, float(points * n_space)),
        out_shape=(
            jax.ShapeDtypeStruct((n_blk, freqs, 2, points), jnp.bfloat16),
            jax.ShapeDtypeStruct((32, freqs), jnp.float32),
        ),
        in_specs=[in_hbm] * 3,
        out_specs=(in_vmem, in_vmem),
        scratch_shapes=[
            pltpu.VMEM((CHUNKS, HOP, width), jnp.float32),
            pltpu.VMEM((CHUNKS, HOP, width), jnp.float32),
            pltpu.VMEM((1, points), jnp.float32),
            pltpu.VMEM((2 * half, 2 * HOP), jnp.bfloat16),
            pltpu.VMEM((2, 2 * half, LANES), jnp.float32),
            pltpu.VMEM((CHUNKS, n_blk + 1, HOP, width), jnp.bfloat16),
            pltpu.VMEM((n_blk + 1, 1, points), jnp.float32),
            pltpu.VMEM((n_blk, half, width), jnp.float32),
            pltpu.VMEM((kinds, freqs, LANES), jnp.float32),
            pltpu.VMEM((n_space, 1, kinds * freqs), jnp.float32),
            dma((CHUNKS,)), dma((CHUNKS,)), dma(()),
            dma((CHUNKS,)), dma((CHUNKS,)), dma((CHUNKS,)), dma((CHUNKS,)), dma((CHUNKS,)), dma((CHUNKS,)),
            dma((3,)), dma((3,)), dma((n_space,)), dma((n_space,)),
        ],
        compiler_params=pltpu.CompilerParams(
            collective_id=0, has_side_effects=True, vmem_limit_bytes=52 * 1024 * 1024
        ),
    )(pressure, final_steps, weights.reshape(1, points))
    spectra, csd = pl.pallas_call(
        finish,
        out_shape=(
            jax.ShapeDtypeStruct(spectra.shape, spectra.dtype),
            jax.ShapeDtypeStruct(csd.shape, csd.dtype),
        ),
        in_specs=[pl.BlockSpec(memory_space=pl.ANY)] * 2,
        out_specs=(in_hbm, in_hbm),
        scratch_shapes=[dma((2,))],
        compiler_params=pltpu.CompilerParams(vmem_limit_bytes=1024 * 1024),
    )(spectra, csd)
    csd = csd.reshape(2, 4, 4, freqs).transpose(0, 3, 1, 2)
    return spectra, csd


def solution(mesh):
    n_space, n_blk = mesh.shape["space"], mesh.shape["blk"]
    return jax.shard_map(
        functools.partial(local, n_space, n_blk),
        mesh=mesh,
        in_specs=(P("blk", "space"), P(None, "space"), P("space")),
        out_specs=(P(None, "blk", None, "space"), P(None, "blk", None, None)),
        check_vma=False,
    )
```

```python
import functools
import math

import jax
import jax.numpy as jnp
from jax import lax
from jax.experimental import pallas as pl
from jax.experimental.pallas import tpu as pltpu
from jax.sharding import PartitionSpec as P

HOP = 128
LANES = 128
CHUNKS = 8
AHEAD = 3
MESH = pl.DeviceIdType.MESH


def make_table(rows, freqs, group):
    blen = 2 * HOP
    row = lax.broadcasted_iota(jnp.int32, (rows, blen), 0)
    t = lax.broadcasted_iota(jnp.int32, (rows, blen), 1)
    mixed = row >= 2 * freqs
    inner = jnp.where(mixed, row - 2 * freqs, row)
    k = group * freqs + jnp.where(mixed, lax.div(inner, 2), lax.rem(inner, freqs))
    part = jnp.where(mixed, lax.rem(inner, 2), lax.div(inner, freqs))
    step = 2.0 * math.pi / blen
    phase = lax.rem(k * t + part * (blen // 4), blen)
    table = jnp.cos(phase.astype(jnp.float32) * step) * (1.0 / math.sqrt(3.0 * blen / 8.0))
    hann = 0.5 - 0.5 * jnp.cos(t[:8].astype(jnp.float32) * step)
    return table.astype(jnp.bfloat16).astype(jnp.float32) * hann[:1]


def each(first, last, body):
    if last - first <= 8:
        for index in range(first, last):
            body(index)
    else:
        pl.loop(first, last)(body)


PAIRS = [(i, j) for i in range(4) for j in range(i, 4)]
CROSS = [(i, j) for i in range(4) for j in range(i + 1, 4)]


def kernel(
    n_space, n_blk, count,
    p_ref, f_ref, w_ref, spec_ref, csd_ref,
    p_buf, f_buf, w_buf, t_buf, edges, ranges, sums, x, acc, rows,
    p_sem, f_sem, w_sem,
    across_send, across_recv, core_send, core_recv, relay_send, relay_recv,
    sum_send, sum_recv, csd_send, csd_recv,
):
    s, q = lax.axis_index("space"), lax.axis_index("blk")
    width = p_buf.shape[2]
    half = t_buf.shape[0] // 2
    freqs = half // 2
    beside = q + 1 - 2 * (q % 2)
    across = (q + 2) % 4
    diagonal = beside + 2 - 4 * (beside // 2)

    def columns(c):
        return pl.ds(pl.multiple_of(c * width, width), width)

    def load(source, target, sem, c):
        return pltpu.make_async_copy(source.at[:, columns(c)], target.at[c], sem.at[c])

    weight_copy = pltpu.make_async_copy(w_ref, w_buf, w_sem)

    barrier = pltpu.get_barrier_semaphore()
    for other in (across, beside, diagonal):
        pl.semaphore_signal(barrier, inc=1, device_id=(s, other), device_id_type=MESH)

    def greet(offset):
        pl.semaphore_signal(barrier, inc=1, device_id=((s + offset) % n_space, q), device_id_type=MESH)

    each(1, n_space, greet)

    for c in range(CHUNKS):
        load(p_ref, p_buf, p_sem, c).start()
    weight_copy.start()
    for c in range(CHUNKS):
        load(f_ref, f_buf, f_sem, c).start()

    def centre(source, target, c, slot):
        values = source[c]
        total = jnp.sum(values, axis=0, keepdims=True)
        sums[slot, :, columns(c)] = total
        target[...] = (values - total * (1.0 / HOP)).astype(jnp.bfloat16)

    def send(ref, index, send_sem, recv_sem, other):
        return pltpu.make_async_remote_copy(
            src_ref=ref.at[index], dst_ref=ref.at[index], send_sem=send_sem, recv_sem=recv_sem,
            device_id=(s, other), device_id_type=MESH,
        )

    def sum_copy(which, owner):
        return send(sums, owner, sum_send.at[which], sum_recv.at[which], (across, beside, diagonal)[which])

    def across_copy(c, owner):
        return send(ranges, (c, owner), across_send.at[c], across_recv.at[c], across)

    def core_copy(c, owner):
        return send(ranges, (c, owner), core_send.at[c], core_recv.at[c], beside)

    def relay_copy(c, owner):
        return send(ranges, (c, owner), relay_send.at[c], relay_recv.at[c], beside)

    def prepare(c):
        load(p_ref, p_buf, p_sem, c).wait()
        centre(p_buf, ranges.at[c, q], c, q)

    def share(c):
        across_copy(c, q).start()
        core_copy(c, q).start()

    prepare(0)
    pl.semaphore_wait(barrier, 3 + n_space - 1)
    share(0)
    prepare(1)
    share(1)
    pl.loop(2, CHUNKS)(prepare)
    for which in range(3):
        sum_copy(which, q).start()
    for c in range(2, AHEAD):
        share(c)

    @pl.loop(0, CHUNKS)
    def _(c):
        load(f_ref, f_buf, f_sem, c).wait()
        centre(f_buf, ranges.at[c, n_blk], c, n_blk)

    acc[...] = jnp.zeros_like(acc)
    table = make_table(2 * half, freqs, q)
    t_buf[...] = table.astype(jnp.bfloat16)
    for side in range(2):
        total = jnp.sum(table[:, side * HOP:(side + 1) * HOP], axis=1, keepdims=True)
        edges[side] = jnp.broadcast_to(total, edges.shape[1:])
    weight_copy.wait()
    for which, owner in enumerate((across, beside, diagonal)):
        sum_copy(which, owner).wait_recv()

    def coefficients(c, first, last):
        before, after = (jnp.tile(edges[side, first:last, :], (1, width // LANES)) for side in range(2))
        parts = [sums[r, :, columns(c)] for r in range(n_blk + 1)]
        mean = sum(parts[1:], parts[0]) * (1.0 / (HOP * (n_blk + 1)))
        offsets = [part * (1.0 / HOP) - mean for part in parts]
        for b in range(n_blk):
            pair = ranges[c, b:b + 2].reshape(2 * HOP, width)
            value = jnp.dot(t_buf[first:last, :], pair, preferred_element_type=jnp.float32)
            yield b, (value + (before * offsets[b] + after * offsets[b + 1])).astype(jnp.bfloat16)

    def keep(b, value):
        x[b] = value.astype(jnp.float32)

    def write(c, b, value):
        spec_ref[b, :, :, columns(c)] = value.reshape(freqs, 2, width)

    def accumulate(c):
        for g in range(freqs // 8):
            low, high = slice(8 * g, 8 * g + 8), slice(freqs + 8 * g, freqs + 8 * g + 8)
            totals = [acc[m, low, :] for m in range(len(PAIRS) + len(CROSS))]
            for tile in range(width // LANES):
                lanes = slice(tile * LANES, (tile + 1) * LANES)
                weight = w_buf[:, pl.ds(pl.multiple_of(c * width + tile * LANES, LANES), LANES)]
                re = [x[b, low, lanes] for b in range(n_blk)]
                im = [x[b, high, lanes] for b in range(n_blk)]
                re_w = [value * weight for value in re]
                im_w = [value * weight for value in im]
                for m, (i, j) in enumerate(PAIRS):
                    totals[m] += re_w[i] * re[j] + im_w[i] * im[j]
                for m, (i, j) in enumerate(CROSS):
                    totals[len(PAIRS) + m] += im_w[i] * re[j] - re_w[i] * im[j]
            for m, total in enumerate(totals):
                acc[m, low, :] = total

    def receive(c):
        across_copy(c, across).wait_recv()
        relay_copy(c, across).start()

    def receive_relayed(c):
        core_copy(c, beside).wait_recv()
        relay_copy(c, diagonal).wait_recv()

    receive(0)
    share(AHEAD)

    @pl.loop(1, CHUNKS)
    def _(c):
        receive(c)

        @pl.when(c + AHEAD < CHUNKS)
        def _():
            share(c + AHEAD)

        receive_relayed(c - 1)
        for b, value in coefficients(c - 1, 0, 2 * half):
            keep(b, value[:half])
            write(c - 1, b, value[half:])
        accumulate(c - 1)

    receive_relayed(CHUNKS - 1)
    for b, value in coefficients(CHUNKS - 1, 0, half):
        keep(b, value)
    accumulate(CHUNKS - 1)

    flat = acc[...].reshape(-1, LANES)
    rows[s] = jnp.sum(flat.T, axis=0, keepdims=True)

    def row_copy(offset, owner, peer):
        return pltpu.make_async_remote_copy(
            src_ref=rows.at[owner], dst_ref=rows.at[owner],
            send_sem=csd_send.at[offset], recv_sem=csd_recv.at[owner],
            device_id=(peer, q), device_id_type=MESH,
        )

    each(1, n_space, lambda offset: row_copy(offset, s, (s + offset) % n_space).start())
    for b, value in coefficients(CHUNKS - 1, half, 2 * half):
        write(CHUNKS - 1, b, value)

    def arrived(offset):
        peer = (s + offset) % n_space
        row_copy(offset, peer, peer).wait_recv()

    each(1, n_space, arrived)
    total = jnp.sum(rows[...], axis=0) * (1.0 / count)
    csd_ref[...] = jnp.zeros_like(csd_ref)
    for m, (i, j) in enumerate(PAIRS + CROSS):
        line = total[:, m * freqs:(m + 1) * freqs]
        if m < len(PAIRS):
            for row in {4 * i + j, 4 * j + i}:
                csd_ref[row:row + 1, :] = line
        else:
            csd_ref[16 + 4 * i + j:17 + 4 * i + j, :] = line
            csd_ref[16 + 4 * j + i:17 + 4 * j + i, :] = -line

    for which in range(3):
        sum_copy(which, q).wait_send()
    for c in range(CHUNKS):
        across_copy(c, q).wait_send()
        core_copy(c, q).wait_send()
        relay_copy(c, across).wait_send()
    each(1, n_space, lambda offset: row_copy(offset, s, (s + offset) % n_space).wait_send())


def finish(spec_ref, csd_ref, spec_out, csd_out, sems):
    copies = [
        pltpu.make_async_copy(spec_ref, spec_out, sems.at[0]),
        pltpu.make_async_copy(csd_ref, csd_out, sems.at[1]),
    ]
    for copy in copies:
        copy.start()
    for copy in copies:
        copy.wait()


def local(n_space, n_blk, pressure, final_steps, weights):
    points = pressure.shape[1]
    width = points // CHUNKS
    freqs = HOP // n_blk
    half = 2 * freqs
    kinds = len(PAIRS) + len(CROSS)
    dma = pltpu.SemaphoreType.DMA
    in_hbm = pl.BlockSpec(memory_space=pltpu.HBM)
    in_vmem = pl.BlockSpec(memory_space=pltpu.VMEM)
    spectra, csd = pl.pallas_call(
        functools.partial(kernel, n_space, n_blk, float(points * n_space)),
        out_shape=(
            jax.ShapeDtypeStruct((n_blk, freqs, 2, points), jnp.bfloat16),
            jax.ShapeDtypeStruct((32, freqs), jnp.float32),
        ),
        in_specs=[in_hbm] * 3,
        out_specs=(in_vmem, in_vmem),
        scratch_shapes=[
            pltpu.VMEM((CHUNKS, HOP, width), jnp.float32),
            pltpu.VMEM((CHUNKS, HOP, width), jnp.float32),
            pltpu.VMEM((1, points), jnp.float32),
            pltpu.VMEM((2 * half, 2 * HOP), jnp.bfloat16),
            pltpu.VMEM((2, 2 * half, LANES), jnp.float32),
            pltpu.VMEM((CHUNKS, n_blk + 1, HOP, width), jnp.bfloat16),
            pltpu.VMEM((n_blk + 1, 1, points), jnp.float32),
            pltpu.VMEM((n_blk, half, width), jnp.float32),
            pltpu.VMEM((kinds, freqs, LANES), jnp.float32),
            pltpu.VMEM((n_space, 1, kinds * freqs), jnp.float32),
            dma((CHUNKS,)), dma((CHUNKS,)), dma(()),
            dma((CHUNKS,)), dma((CHUNKS,)), dma((CHUNKS,)), dma((CHUNKS,)), dma((CHUNKS,)), dma((CHUNKS,)),
            dma((3,)), dma((3,)), dma((n_space,)), dma((n_space,)),
        ],
        compiler_params=pltpu.CompilerParams(
            collective_id=0, has_side_effects=True, vmem_limit_bytes=52 * 1024 * 1024
        ),
    )(pressure, final_steps, weights.reshape(1, points))
    spectra, csd = pl.pallas_call(
        finish,
        out_shape=(
            jax.ShapeDtypeStruct(spectra.shape, spectra.dtype),
            jax.ShapeDtypeStruct(csd.shape, csd.dtype),
        ),
        in_specs=[pl.BlockSpec(memory_space=pl.ANY)] * 2,
        out_specs=(in_hbm, in_hbm),
        scratch_shapes=[dma((2,))],
        compiler_params=pltpu.CompilerParams(vmem_limit_bytes=1024 * 1024),
    )(spectra, csd)
    csd = csd.reshape(2, 4, 4, freqs).transpose(0, 3, 1, 2)
    return spectra, csd


def solution(mesh):
    n_space, n_blk = mesh.shape["space"], mesh.shape["blk"]
    return jax.shard_map(
        functools.partial(local, n_space, n_blk),
        mesh=mesh,
        in_specs=(P("blk", "space"), P(None, "space"), P("space")),
        out_specs=(P(None, "blk", None, "space"), P(None, "blk", None, None)),
        check_vma=False,
    )
```

```python
import functools
import math

import jax
import jax.numpy as jnp
from jax import lax
from jax.experimental import pallas as pl
from jax.experimental.pallas import tpu as pltpu
from jax.sharding import PartitionSpec as P

HOP = 128
LANES = 128
CHUNKS = 16
MESH = pl.DeviceIdType.MESH


def make_table(rows, freqs, group):
    blen = 2 * HOP
    row = lax.broadcasted_iota(jnp.int32, (rows, blen), 0)
    t = lax.broadcasted_iota(jnp.int32, (rows, blen), 1)
    mixed = row >= 2 * freqs
    inner = jnp.where(mixed, row - 2 * freqs, row)
    k = group * freqs + jnp.where(mixed, lax.div(inner, 2), lax.rem(inner, freqs))
    part = jnp.where(mixed, lax.rem(inner, 2), lax.div(inner, freqs))
    step = 2.0 * math.pi / blen
    phase = lax.rem(k * t + part * (blen // 4), blen)
    table = jnp.cos(phase.astype(jnp.float32) * step) * (1.0 / math.sqrt(3.0 * blen / 8.0))
    hann = 0.5 - 0.5 * jnp.cos(t[:8].astype(jnp.float32) * step)
    return table.astype(jnp.bfloat16).astype(jnp.float32) * hann[:1]


def each(first, last, body):
    if last - first <= 8:
        for index in range(first, last):
            body(index)
    else:
        pl.loop(first, last)(body)


PAIRS = [(i, j) for i in range(4) for j in range(i, 4)]
CROSS = [(i, j) for i in range(4) for j in range(i + 1, 4)]


def kernel(
    n_space, n_blk, count,
    p_ref, f_ref, w_ref, spec_ref, csd_ref,
    p_buf, f_buf, w_buf, t_buf, edges, ranges, sums, x, acc, rows,
    p_sem, f_sem, w_sem,
    across_send, across_recv, core_send, core_recv, relay_send, relay_recv,
    sum_send, sum_recv, csd_send, csd_recv,
):
    s, q = lax.axis_index("space"), lax.axis_index("blk")
    width = p_buf.shape[2]
    half = t_buf.shape[0] // 2
    freqs = half // 2
    beside = q + 1 - 2 * (q % 2)
    across = (q + 2) % 4
    diagonal = beside + 2 - 4 * (beside // 2)

    def columns(c):
        return pl.ds(pl.multiple_of(c * width, width), width)

    def load(source, target, sem, c):
        return pltpu.make_async_copy(source.at[:, columns(c)], target.at[c], sem.at[c])

    weight_copy = pltpu.make_async_copy(w_ref, w_buf, w_sem)

    barrier = pltpu.get_barrier_semaphore()
    for other in (across, beside, diagonal):
        pl.semaphore_signal(barrier, inc=1, device_id=(s, other), device_id_type=MESH)

    def greet(offset):
        pl.semaphore_signal(barrier, inc=1, device_id=((s + offset) % n_space, q), device_id_type=MESH)

    each(1, n_space, greet)

    for c in range(CHUNKS):
        load(p_ref, p_buf, p_sem, c).start()
    weight_copy.start()
    for c in range(CHUNKS):
        load(f_ref, f_buf, f_sem, c).start()

    def centre(source, target, c, slot):
        values = source[c]
        total = jnp.sum(values, axis=0, keepdims=True)
        sums[slot, :, columns(c)] = total
        target[...] = (values - total * (1.0 / HOP)).astype(jnp.bfloat16)

    def send(ref, index, send_sem, recv_sem, other):
        return pltpu.make_async_remote_copy(
            src_ref=ref.at[index], dst_ref=ref.at[index], send_sem=send_sem, recv_sem=recv_sem,
            device_id=(s, other), device_id_type=MESH,
        )

    def sum_copy(which, owner):
        return send(sums, owner, sum_send.at[which], sum_recv.at[which], (across, beside, diagonal)[which])

    def across_copy(c, owner):
        return send(ranges, (c, owner), across_send.at[c], across_recv.at[c], across)

    def core_copy(c, owner):
        return send(ranges, (c, owner), core_send.at[c], core_recv.at[c], beside)

    def relay_copy(c, owner):
        return send(ranges, (c, owner), relay_send.at[c], relay_recv.at[c], beside)

    def prepare(c):
        load(p_ref, p_buf, p_sem, c).wait()
        centre(p_buf, ranges.at[c, q], c, q)

    def share(c):
        across_copy(c, q).start()
        core_copy(c, q).start()

    prepare(0)
    pl.semaphore_wait(barrier, 3 + n_space - 1)
    share(0)
    prepare(1)
    share(1)
    pl.loop(2, CHUNKS)(prepare)
    for which in range(3):
        sum_copy(which, q).start()
    for c in range(2, CHUNKS):
        share(c)

    @pl.loop(0, CHUNKS)
    def _(c):
        load(f_ref, f_buf, f_sem, c).wait()
        centre(f_buf, ranges.at[c, n_blk], c, n_blk)

    acc[...] = jnp.zeros_like(acc)
    table = make_table(2 * half, freqs, q)
    t_buf[...] = table.astype(jnp.bfloat16)
    for side in range(2):
        total = jnp.sum(table[:, side * HOP:(side + 1) * HOP], axis=1, keepdims=True)
        edges[side] = jnp.broadcast_to(total, edges.shape[1:])
    weight_copy.wait()
    for which, owner in enumerate((across, beside, diagonal)):
        sum_copy(which, owner).wait_recv()

    def coefficients(c, first, last):
        before, after = (jnp.tile(edges[side, first:last, :], (1, width // LANES)) for side in range(2))
        parts = [sums[r, :, columns(c)] for r in range(n_blk + 1)]
        mean = sum(parts[1:], parts[0]) * (1.0 / (HOP * (n_blk + 1)))
        offsets = [part * (1.0 / HOP) - mean for part in parts]
        for b in range(n_blk):
            pair = ranges[c, b:b + 2].reshape(2 * HOP, width)
            value = jnp.dot(t_buf[first:last, :], pair, preferred_element_type=jnp.float32)
            yield b, (value + (before * offsets[b] + after * offsets[b + 1])).astype(jnp.bfloat16)

    def keep(b, value):
        x[b] = value.astype(jnp.float32)

    def write(c, b, value):
        spec_ref[b, :, :, columns(c)] = value.reshape(freqs, 2, width)

    def accumulate(c):
        for g in range(freqs // 8):
            low, high = slice(8 * g, 8 * g + 8), slice(freqs + 8 * g, freqs + 8 * g + 8)
            totals = [acc[m, low, :] for m in range(len(PAIRS) + len(CROSS))]
            for tile in range(width // LANES):
                lanes = slice(tile * LANES, (tile + 1) * LANES)
                weight = w_buf[:, pl.ds(pl.multiple_of(c * width + tile * LANES, LANES), LANES)]
                re = [x[b, low, lanes] for b in range(n_blk)]
                im = [x[b, high, lanes] for b in range(n_blk)]
                re_w = [value * weight for value in re]
                im_w = [value * weight for value in im]
                for m, (i, j) in enumerate(PAIRS):
                    totals[m] += re_w[i] * re[j] + im_w[i] * im[j]
                for m, (i, j) in enumerate(CROSS):
                    totals[len(PAIRS) + m] += im_w[i] * re[j] - re_w[i] * im[j]
            for m, total in enumerate(totals):
                acc[m, low, :] = total

    def receive(c):
        across_copy(c, across).wait_recv()
        relay_copy(c, across).start()

    def receive_relayed(c):
        core_copy(c, beside).wait_recv()
        relay_copy(c, diagonal).wait_recv()

    receive(0)

    @pl.loop(1, CHUNKS)
    def _(c):
        receive(c)
        receive_relayed(c - 1)
        for b, value in coefficients(c - 1, 0, 2 * half):
            keep(b, value[:half])
            write(c - 1, b, value[half:])
        accumulate(c - 1)

    receive_relayed(CHUNKS - 1)
    for b, value in coefficients(CHUNKS - 1, 0, half):
        keep(b, value)
    accumulate(CHUNKS - 1)

    flat = acc[...].reshape(-1, LANES)
    rows[s] = jnp.sum(flat.T, axis=0, keepdims=True)

    def row_copy(offset, owner, peer):
        return pltpu.make_async_remote_copy(
            src_ref=rows.at[owner], dst_ref=rows.at[owner],
            send_sem=csd_send.at[offset], recv_sem=csd_recv.at[owner],
            device_id=(peer, q), device_id_type=MESH,
        )

    each(1, n_space, lambda offset: row_copy(offset, s, (s + offset) % n_space).start())
    for b, value in coefficients(CHUNKS - 1, half, 2 * half):
        write(CHUNKS - 1, b, value)

    def arrived(offset):
        peer = (s + offset) % n_space
        row_copy(offset, peer, peer).wait_recv()

    each(1, n_space, arrived)
    total = jnp.sum(rows[...], axis=0) * (1.0 / count)
    csd_ref[...] = jnp.zeros_like(csd_ref)
    for m, (i, j) in enumerate(PAIRS + CROSS):
        line = total[:, m * freqs:(m + 1) * freqs]
        if m < len(PAIRS):
            for row in {4 * i + j, 4 * j + i}:
                csd_ref[row:row + 1, :] = line
        else:
            csd_ref[16 + 4 * i + j:17 + 4 * i + j, :] = line
            csd_ref[16 + 4 * j + i:17 + 4 * j + i, :] = -line

    for which in range(3):
        sum_copy(which, q).wait_send()
    for c in range(CHUNKS):
        across_copy(c, q).wait_send()
        core_copy(c, q).wait_send()
        relay_copy(c, across).wait_send()
    each(1, n_space, lambda offset: row_copy(offset, s, (s + offset) % n_space).wait_send())


def finish(spec_ref, csd_ref, spec_out, csd_out, sems):
    copies = [
        pltpu.make_async_copy(spec_ref, spec_out, sems.at[0]),
        pltpu.make_async_copy(csd_ref, csd_out, sems.at[1]),
    ]
    for copy in copies:
        copy.start()
    for copy in copies:
        copy.wait()


def local(n_space, n_blk, pressure, final_steps, weights):
    points = pressure.shape[1]
    width = points // CHUNKS
    freqs = HOP // n_blk
    half = 2 * freqs
    kinds = len(PAIRS) + len(CROSS)
    dma = pltpu.SemaphoreType.DMA
    in_hbm = pl.BlockSpec(memory_space=pltpu.HBM)
    in_vmem = pl.BlockSpec(memory_space=pltpu.VMEM)
    spectra, csd = pl.pallas_call(
        functools.partial(kernel, n_space, n_blk, float(points * n_space)),
        out_shape=(
            jax.ShapeDtypeStruct((n_blk, freqs, 2, points), jnp.bfloat16),
            jax.ShapeDtypeStruct((32, freqs), jnp.float32),
        ),
        in_specs=[in_hbm] * 3,
        out_specs=(in_vmem, in_vmem),
        scratch_shapes=[
            pltpu.VMEM((CHUNKS, HOP, width), jnp.float32),
            pltpu.VMEM((CHUNKS, HOP, width), jnp.float32),
            pltpu.VMEM((1, points), jnp.float32),
            pltpu.VMEM((2 * half, 2 * HOP), jnp.bfloat16),
            pltpu.VMEM((2, 2 * half, LANES), jnp.float32),
            pltpu.VMEM((CHUNKS, n_blk + 1, HOP, width), jnp.bfloat16),
            pltpu.VMEM((n_blk + 1, 1, points), jnp.float32),
            pltpu.VMEM((n_blk, half, width), jnp.float32),
            pltpu.VMEM((kinds, freqs, LANES), jnp.float32),
            pltpu.VMEM((n_space, 1, kinds * freqs), jnp.float32),
            dma((CHUNKS,)), dma((CHUNKS,)), dma(()),
            dma((CHUNKS,)), dma((CHUNKS,)), dma((CHUNKS,)), dma((CHUNKS,)), dma((CHUNKS,)), dma((CHUNKS,)),
            dma((3,)), dma((3,)), dma((n_space,)), dma((n_space,)),
        ],
        compiler_params=pltpu.CompilerParams(
            collective_id=0, has_side_effects=True, vmem_limit_bytes=52 * 1024 * 1024
        ),
    )(pressure, final_steps, weights.reshape(1, points))
    spectra, csd = pl.pallas_call(
        finish,
        out_shape=(
            jax.ShapeDtypeStruct(spectra.shape, spectra.dtype),
            jax.ShapeDtypeStruct(csd.shape, csd.dtype),
        ),
        in_specs=[pl.BlockSpec(memory_space=pl.ANY)] * 2,
        out_specs=(in_hbm, in_hbm),
        scratch_shapes=[dma((2,))],
        compiler_params=pltpu.CompilerParams(vmem_limit_bytes=1024 * 1024),
    )(spectra, csd)
    csd = csd.reshape(2, 4, 4, freqs).transpose(0, 3, 1, 2)
    return spectra, csd


def solution(mesh):
    n_space, n_blk = mesh.shape["space"], mesh.shape["blk"]
    return jax.shard_map(
        functools.partial(local, n_space, n_blk),
        mesh=mesh,
        in_specs=(P("blk", "space"), P(None, "space"), P("space")),
        out_specs=(P(None, "blk", None, "space"), P(None, "blk", None, None)),
        check_vma=False,
    )
```

```python
import functools
import math

import jax
import jax.numpy as jnp
from jax import lax
from jax.experimental import pallas as pl
from jax.experimental.pallas import tpu as pltpu
from jax.sharding import PartitionSpec as P

HOP = 128
LANES = 128
CHUNKS = 4
MESH = pl.DeviceIdType.MESH


def make_table(rows, freqs, group):
    blen = 2 * HOP
    row = lax.broadcasted_iota(jnp.int32, (rows, blen), 0)
    t = lax.broadcasted_iota(jnp.int32, (rows, blen), 1)
    mixed = row >= 2 * freqs
    inner = jnp.where(mixed, row - 2 * freqs, row)
    k = group * freqs + jnp.where(mixed, lax.div(inner, 2), lax.rem(inner, freqs))
    part = jnp.where(mixed, lax.rem(inner, 2), lax.div(inner, freqs))
    step = 2.0 * math.pi / blen
    phase = lax.rem(k * t + part * (blen // 4), blen)
    table = jnp.cos(phase.astype(jnp.float32) * step) * (1.0 / math.sqrt(3.0 * blen / 8.0))
    hann = 0.5 - 0.5 * jnp.cos(t[:8].astype(jnp.float32) * step)
    return table.astype(jnp.bfloat16).astype(jnp.float32) * hann[:1]


def each(first, last, body):
    if last - first <= 8:
        for index in range(first, last):
            body(index)
    else:
        pl.loop(first, last)(body)


PAIRS = [(i, j) for i in range(4) for j in range(i, 4)]
CROSS = [(i, j) for i in range(4) for j in range(i + 1, 4)]


def kernel(
    n_space, n_blk, count,
    p_ref, f_ref, w_ref, spec_ref, csd_ref,
    p_buf, f_buf, w_buf, t_buf, edges, ranges, sums, x, acc, rows,
    p_sem, f_sem, w_sem,
    across_send, across_recv, core_send, core_recv, relay_send, relay_recv,
    sum_send, sum_recv, csd_send, csd_recv,
):
    s, q = lax.axis_index("space"), lax.axis_index("blk")
    width = p_buf.shape[2]
    half = t_buf.shape[0] // 2
    freqs = half // 2
    beside = q + 1 - 2 * (q % 2)
    across = (q + 2) % 4
    diagonal = beside + 2 - 4 * (beside // 2)

    def columns(c):
        return pl.ds(pl.multiple_of(c * width, width), width)

    def load(source, target, sem, c):
        return pltpu.make_async_copy(source.at[:, columns(c)], target.at[c], sem.at[c])

    weight_copy = pltpu.make_async_copy(w_ref, w_buf, w_sem)

    barrier = pltpu.get_barrier_semaphore()
    for other in (across, beside, diagonal):
        pl.semaphore_signal(barrier, inc=1, device_id=(s, other), device_id_type=MESH)

    def greet(offset):
        pl.semaphore_signal(barrier, inc=1, device_id=((s + offset) % n_space, q), device_id_type=MESH)

    each(1, n_space, greet)

    for c in range(CHUNKS):
        load(p_ref, p_buf, p_sem, c).start()
    weight_copy.start()
    for c in range(CHUNKS):
        load(f_ref, f_buf, f_sem, c).start()

    def centre(source, target, c, slot):
        values = source[c]
        total = jnp.sum(values, axis=0, keepdims=True)
        sums[slot, :, columns(c)] = total
        target[...] = (values - total * (1.0 / HOP)).astype(jnp.bfloat16)

    def send(ref, index, send_sem, recv_sem, other):
        return pltpu.make_async_remote_copy(
            src_ref=ref.at[index], dst_ref=ref.at[index], send_sem=send_sem, recv_sem=recv_sem,
            device_id=(s, other), device_id_type=MESH,
        )

    def sum_copy(which, owner):
        return send(sums, owner, sum_send.at[which], sum_recv.at[which], (across, beside, diagonal)[which])

    def across_copy(c, owner):
        return send(ranges, (c, owner), across_send.at[c], across_recv.at[c], across)

    def core_copy(c, owner):
        return send(ranges, (c, owner), core_send.at[c], core_recv.at[c], beside)

    def relay_copy(c, owner):
        return send(ranges, (c, owner), relay_send.at[c], relay_recv.at[c], beside)

    def prepare(c):
        load(p_ref, p_buf, p_sem, c).wait()
        centre(p_buf, ranges.at[c, q], c, q)

    def share(c):
        across_copy(c, q).start()
        core_copy(c, q).start()

    prepare(0)
    pl.semaphore_wait(barrier, 3 + n_space - 1)
    share(0)
    prepare(1)
    share(1)
    pl.loop(2, CHUNKS)(prepare)
    for which in range(3):
        sum_copy(which, q).start()
    for c in range(2, CHUNKS):
        share(c)

    @pl.loop(0, CHUNKS)
    def _(c):
        load(f_ref, f_buf, f_sem, c).wait()
        centre(f_buf, ranges.at[c, n_blk], c, n_blk)

    acc[...] = jnp.zeros_like(acc)
    table = make_table(2 * half, freqs, q)
    t_buf[...] = table.astype(jnp.bfloat16)
    for side in range(2):
        total = jnp.sum(table[:, side * HOP:(side + 1) * HOP], axis=1, keepdims=True)
        edges[side] = jnp.broadcast_to(total, edges.shape[1:])
    weight_copy.wait()
    for which, owner in enumerate((across, beside, diagonal)):
        sum_copy(which, owner).wait_recv()

    def coefficients(c, first, last):
        before, after = (jnp.tile(edges[side, first:last, :], (1, width // LANES)) for side in range(2))
        parts = [sums[r, :, columns(c)] for r in range(n_blk + 1)]
        mean = sum(parts[1:], parts[0]) * (1.0 / (HOP * (n_blk + 1)))
        offsets = [part * (1.0 / HOP) - mean for part in parts]
        for b in range(n_blk):
            pair = ranges[c, b:b + 2].reshape(2 * HOP, width)
            value = jnp.dot(t_buf[first:last, :], pair, preferred_element_type=jnp.float32)
            yield b, (value + (before * offsets[b] + after * offsets[b + 1])).astype(jnp.bfloat16)

    def keep(b, value):
        x[b] = value.astype(jnp.float32)

    def write(c, b, value):
        spec_ref[b, :, :, columns(c)] = value.reshape(freqs, 2, width)

    def accumulate(c):
        for g in range(freqs // 8):
            low, high = slice(8 * g, 8 * g + 8), slice(freqs + 8 * g, freqs + 8 * g + 8)
            totals = [acc[m, low, :] for m in range(len(PAIRS) + len(CROSS))]
            for tile in range(width // LANES):
                lanes = slice(tile * LANES, (tile + 1) * LANES)
                weight = w_buf[:, pl.ds(pl.multiple_of(c * width + tile * LANES, LANES), LANES)]
                re = [x[b, low, lanes] for b in range(n_blk)]
                im = [x[b, high, lanes] for b in range(n_blk)]
                re_w = [value * weight for value in re]
                im_w = [value * weight for value in im]
                for m, (i, j) in enumerate(PAIRS):
                    totals[m] += re_w[i] * re[j] + im_w[i] * im[j]
                for m, (i, j) in enumerate(CROSS):
                    totals[len(PAIRS) + m] += im_w[i] * re[j] - re_w[i] * im[j]
            for m, total in enumerate(totals):
                acc[m, low, :] = total

    def receive(c):
        across_copy(c, across).wait_recv()
        relay_copy(c, across).start()

    def receive_relayed(c):
        core_copy(c, beside).wait_recv()
        relay_copy(c, diagonal).wait_recv()

    receive(0)

    @pl.loop(1, CHUNKS)
    def _(c):
        receive(c)
        receive_relayed(c - 1)
        for b, value in coefficients(c - 1, 0, 2 * half):
            keep(b, value[:half])
            write(c - 1, b, value[half:])
        accumulate(c - 1)

    receive_relayed(CHUNKS - 1)
    for b, value in coefficients(CHUNKS - 1, 0, half):
        keep(b, value)
    accumulate(CHUNKS - 1)

    flat = acc[...].reshape(-1, LANES)
    rows[s] = jnp.sum(flat.T, axis=0, keepdims=True)

    def row_copy(offset, owner, peer):
        return pltpu.make_async_remote_copy(
            src_ref=rows.at[owner], dst_ref=rows.at[owner],
            send_sem=csd_send.at[offset], recv_sem=csd_recv.at[owner],
            device_id=(peer, q), device_id_type=MESH,
        )

    each(1, n_space, lambda offset: row_copy(offset, s, (s + offset) % n_space).start())
    for b, value in coefficients(CHUNKS - 1, half, 2 * half):
        write(CHUNKS - 1, b, value)

    def arrived(offset):
        peer = (s + offset) % n_space
        row_copy(offset, peer, peer).wait_recv()

    each(1, n_space, arrived)
    total = jnp.sum(rows[...], axis=0) * (1.0 / count)
    csd_ref[...] = jnp.zeros_like(csd_ref)
    for m, (i, j) in enumerate(PAIRS + CROSS):
        line = total[:, m * freqs:(m + 1) * freqs]
        if m < len(PAIRS):
            for row in {4 * i + j, 4 * j + i}:
                csd_ref[row:row + 1, :] = line
        else:
            csd_ref[16 + 4 * i + j:17 + 4 * i + j, :] = line
            csd_ref[16 + 4 * j + i:17 + 4 * j + i, :] = -line

    for which in range(3):
        sum_copy(which, q).wait_send()
    for c in range(CHUNKS):
        across_copy(c, q).wait_send()
        core_copy(c, q).wait_send()
        relay_copy(c, across).wait_send()
    each(1, n_space, lambda offset: row_copy(offset, s, (s + offset) % n_space).wait_send())


def finish(spec_ref, csd_ref, spec_out, csd_out, sems):
    copies = [
        pltpu.make_async_copy(spec_ref, spec_out, sems.at[0]),
        pltpu.make_async_copy(csd_ref, csd_out, sems.at[1]),
    ]
    for copy in copies:
        copy.start()
    for copy in copies:
        copy.wait()


def local(n_space, n_blk, pressure, final_steps, weights):
    points = pressure.shape[1]
    width = points // CHUNKS
    freqs = HOP // n_blk
    half = 2 * freqs
    kinds = len(PAIRS) + len(CROSS)
    dma = pltpu.SemaphoreType.DMA
    in_hbm = pl.BlockSpec(memory_space=pltpu.HBM)
    in_vmem = pl.BlockSpec(memory_space=pltpu.VMEM)
    spectra, csd = pl.pallas_call(
        functools.partial(kernel, n_space, n_blk, float(points * n_space)),
        out_shape=(
            jax.ShapeDtypeStruct((n_blk, freqs, 2, points), jnp.bfloat16),
            jax.ShapeDtypeStruct((32, freqs), jnp.float32),
        ),
        in_specs=[in_hbm] * 3,
        out_specs=(in_vmem, in_vmem),
        scratch_shapes=[
            pltpu.VMEM((CHUNKS, HOP, width), jnp.float32),
            pltpu.VMEM((CHUNKS, HOP, width), jnp.float32),
            pltpu.VMEM((1, points), jnp.float32),
            pltpu.VMEM((2 * half, 2 * HOP), jnp.bfloat16),
            pltpu.VMEM((2, 2 * half, LANES), jnp.float32),
            pltpu.VMEM((CHUNKS, n_blk + 1, HOP, width), jnp.bfloat16),
            pltpu.VMEM((n_blk + 1, 1, points), jnp.float32),
            pltpu.VMEM((n_blk, half, width), jnp.float32),
            pltpu.VMEM((kinds, freqs, LANES), jnp.float32),
            pltpu.VMEM((n_space, 1, kinds * freqs), jnp.float32),
            dma((CHUNKS,)), dma((CHUNKS,)), dma(()),
            dma((CHUNKS,)), dma((CHUNKS,)), dma((CHUNKS,)), dma((CHUNKS,)), dma((CHUNKS,)), dma((CHUNKS,)),
            dma((3,)), dma((3,)), dma((n_space,)), dma((n_space,)),
        ],
        compiler_params=pltpu.CompilerParams(
            collective_id=0, has_side_effects=True, vmem_limit_bytes=52 * 1024 * 1024
        ),
    )(pressure, final_steps, weights.reshape(1, points))
    spectra, csd = pl.pallas_call(
        finish,
        out_shape=(
            jax.ShapeDtypeStruct(spectra.shape, spectra.dtype),
            jax.ShapeDtypeStruct(csd.shape, csd.dtype),
        ),
        in_specs=[pl.BlockSpec(memory_space=pl.ANY)] * 2,
        out_specs=(in_hbm, in_hbm),
        scratch_shapes=[dma((2,))],
        compiler_params=pltpu.CompilerParams(vmem_limit_bytes=1024 * 1024),
    )(spectra, csd)
    csd = csd.reshape(2, 4, 4, freqs).transpose(0, 3, 1, 2)
    return spectra, csd


def solution(mesh):
    n_space, n_blk = mesh.shape["space"], mesh.shape["blk"]
    return jax.shard_map(
        functools.partial(local, n_space, n_blk),
        mesh=mesh,
        in_specs=(P("blk", "space"), P(None, "space"), P("space")),
        out_specs=(P(None, "blk", None, "space"), P(None, "blk", None, None)),
        check_vma=False,
    )
```
